32 devices in a mesh: dp: 16 (over z, y, x), tensor: 2 (over core).
Axes of the slice: x: 2, y: 2, z: 4, core: 2. Of those that a mesh axis runs over, the one named last changes fastest.
Arguments:
- block_input: bfloat16 [4096, 1024], P('dp'), may hold values from -6 to 6
- cotangent: bfloat16 [4096, 1024], P('dp'), may hold values from -6 to 6
- seq_lengths: int32 [16, 4], P('dp'), may hold values from 0 to 256, as said below
- ln1_gain: float32 [1024], replicated, may hold values from 0.1 to 1.9
- ln1_bias: float32 [1024], replicated, may hold values from -4 to 4
- w_qkv: bfloat16 [3, 1024, 1024], P(None, None, 'tensor'), may hold values from -0.1875 to 0.1875
- qv_bias: float32 [2, 1024], P(None, 'tensor'), may hold values from -6 to 6
- w_out: bfloat16 [1024, 1024], P('tensor'), may hold values from -0.75 to 0.75
- out_bias: float32 [1024], replicated, may hold values from -6 to 6
- ln2_gain: float32 [1024], replicated, may hold values from 0.1 to 1.9
- ln2_bias: float32 [1024], replicated, may hold values from -4 to 4
- w_fc: bfloat16 [1024, 4096], P(None, 'tensor'), may hold values from -0.1875 to 0.1875
- fc_bias: float32 [4096], P('tensor'), may hold values from -6 to 6
- w_proj: bfloat16 [4096, 1024], P('tensor'), may hold values from -0.09375 to 0.09375
- proj_bias: float32 [1024], replicated, may hold values from -6 to 6
Outputs:
- block_output: bfloat16 [4096, 1024], P('dp')
- input_grad: bfloat16 [4096, 1024], P('dp')
- ln1_gain_grad: float32 [1024], replicated
- ln1_bias_grad: float32 [1024], replicated
- w_qkv_grad: float32 [3, 1024, 1024], P(None, None, 'tensor')
- qv_bias_grad: float32 [2, 1024], P(None, 'tensor')
- w_out_grad: float32 [1024, 1024], P('tensor')
- out_bias_grad: float32 [1024], replicated
- ln2_gain_grad: float32 [1024], replicated
- ln2_bias_grad: float32 [1024], replicated
- w_fc_grad: float32 [1024, 4096], P(None, 'tensor')
- fc_bias_grad: float32 [4096], P('tensor')
- w_proj_grad: float32 [4096, 1024], P('tensor')
- proj_bias_grad: float32 [1024], replicated
The draws below stay inside these ranges and needn't reach their ends.
Inputs may be any that keep to these rules, and one draw needn't show every extreme that they name: `seq_lengths`: row i lists the lengths of the 4 sequences packed in order from the first row of data index i; a row sums to at most 256, the rows after them are padding, lengths may be zero, and in every draw some row holds one sequence of 256 tokens.
All inputs are finite; a program needn't handle non-finite values.
Results may differ from the reference program's by a relative error of at most 0.012.
Values sent between devices are 32-bit elements; how exact they have to be, the bound alone decides.
A program may use at most 192 MiB of HBM per device.

```python
from functools import partial
import jax
import jax.numpy as jnp
from jax import lax

D = 1024
HEADS = 16
HEAD_DIM = 64
FF = 4096
TOK_DEV = 256
SEQ_DEV = 4
TOKENS = 4096
N_DP = 16


def draw_seq_lengths(key, part):
    key = jax.random.fold_in(key, 11)
    first, second, third = jax.random.split(key, 3)
    totals = jax.random.randint(first, (N_DP, 1), TOK_DEV // 4, TOK_DEV + 1)
    cuts = jax.random.randint(second, (N_DP, SEQ_DEV - 1), 0, TOK_DEV + 1)
    cuts = jnp.minimum(jnp.sort(cuts, axis=1), totals)
    bounds = jnp.concatenate([jnp.zeros((N_DP, 1), jnp.int32), cuts, totals], axis=1)
    lengths = bounds[:, 1:] - bounds[:, :-1]
    chosen = jax.random.randint(third, (), 0, N_DP)
    single = jnp.where(jnp.arange(SEQ_DEV) == 0, TOK_DEV, 0).astype(jnp.int32)
    picked = (jnp.arange(N_DP) == chosen)[:, None]
    return jnp.where(picked, single[None, :], lengths).astype(jnp.int32)


def strengthened(array, rng, source, target, parts, factor):
    owner, partner = [(jnp.arange(array.shape[dim]) // (array.shape[dim] // parts)).reshape([-1 if axis == dim else 1 for axis in range(array.ndim)]) for dim in (source, target)]
    chosen = jax.random.permutation(rng, parts)[partner]
    strong = (owner == chosen) | (owner == (partner + parts // 2) % parts)
    return jnp.where(strong, factor * array, array)


def steps_of(own_key, extent, cuts, low, largest):
    def one(dim, blocks):
        steps = jax.random.uniform(jax.random.fold_in(jax.random.fold_in(own_key, 6), dim), (blocks,), jnp.float32, low / len(cuts), largest / len(cuts))
        return jnp.repeat(jnp.exp(steps), extent[dim] // blocks).reshape((-1,) + (1,) * (len(extent) - dim - 1))

    loudness = one(*cuts[0])
    for cut in cuts[1:]:
        loudness = loudness * one(*cut)
    return loudness


def scatter_about(rng, shape, scale, most, shards=(), kind=jnp.bfloat16):
    drawn = scale * jax.random.normal(rng, shape, jnp.float32)
    if shards:
        drawn = drawn * steps_of(rng, shape, shards, -0.22, 0.18)
    return jnp.clip(drawn, -most, most).astype(kind)


def gaussian_with(stream_key, extent, scale, limit, cuts, heavy, kind=jnp.bfloat16):
    entries = scale * jax.random.normal(stream_key, extent, jnp.float32)
    if cuts:
        entries = entries * steps_of(stream_key, extent, cuts, -0.22, 0.18)
    return jnp.clip(strengthened(entries, jax.random.fold_in(stream_key, 3), *heavy), -limit, limit).astype(kind)


def setup_inputs(seed: int = 0) -> dict:
    streams_of = jax.random.split(jax.random.key(seed), 16)
    block_input = scatter_about(streams_of[0], (TOKENS, D), 1.0, 6.0, ((0, 16),))
    cotangent = gaussian_with(streams_of[1], (TOKENS, D), 1.0, 6.0, ((0, 16),), (0, 1, 16, 2.0))
    seq_lengths = draw_seq_lengths(jax.random.fold_in(streams_of[15], 71), 0)
    ln1_gain = jnp.clip(1.0 + 0.18 * jax.random.normal(streams_of[3], (D,), jnp.float32), 0.1, 1.9)
    ln1_bias = scatter_about(streams_of[4], (D,), 0.3, 4.0, (), jnp.float32)
    w_qkv = scatter_about(streams_of[5], (3, D, D), D ** -0.5, 0.1875, ((2, 2),))
    qv_bias = scatter_about(streams_of[6], (2, D), 0.5, 6.0, ((1, 2),), jnp.float32)
    w_out = scatter_about(streams_of[7], (D, D), (D // 16) ** -0.5, 0.75, ((0, 2),))
    out_bias = scatter_about(streams_of[8], (D,), 0.5, 6.0, (), jnp.float32)
    ln2_gain = jnp.clip(1.0 + 0.18 * jax.random.normal(streams_of[9], (D,), jnp.float32), 0.1, 1.9)
    ln2_bias = scatter_about(streams_of[10], (D,), 0.3, 4.0, (), jnp.float32)
    w_fc = scatter_about(streams_of[11], (D, FF), D ** -0.5, 0.1875, ((1, 2),))
    fc_bias = scatter_about(streams_of[12], (FF,), 0.5, 6.0, ((0, 2),), jnp.float32)
    w_proj = scatter_about(streams_of[13], (FF, D), FF ** -0.5, 0.09375, ((0, 2),))
    proj_bias = scatter_about(streams_of[14], (D,), 0.5, 6.0, (), jnp.float32)
    return {"block_input": block_input, "cotangent": cotangent, "seq_lengths": seq_lengths, "ln1_gain": ln1_gain, "ln1_bias": ln1_bias, "w_qkv": w_qkv, "qv_bias": qv_bias, "w_out": w_out, "out_bias": out_bias, "ln2_gain": ln2_gain, "ln2_bias": ln2_bias, "w_fc": w_fc, "fc_bias": fc_bias, "w_proj": w_proj, "proj_bias": proj_bias}


EPS = 1e-05
GELU_SCALE = 0.7978845608028654
SCORE_SCALE = 0.125
HIGH = lax.Precision.HIGHEST

@jax.custom_vjp
def low(v):
    return lax.optimization_barrier(v.astype(jnp.bfloat16)).astype(jnp.float32)

@jax.custom_vjp
def low_back(v):
    return v

def low_keep(v):
    return (low(v), None)

def low_pass(kept, grad):
    return (grad,)

def back_keep(v):
    return (v, None)

def back_low(kept, grad):
    return (low(grad),)
low.defvjp(low_keep, low_pass)
low_back.defvjp(back_keep, back_low)

def layer_norm(values, gain, shift):
    centre = lax.optimization_barrier(jnp.mean(values, axis=-1, keepdims=True))
    centred = values - centre
    spread = lax.optimization_barrier(jnp.mean(centred * centred, axis=-1, keepdims=True))
    return centred * lax.rsqrt(spread + EPS) * gain + shift

def gelu(values):
    return 0.5 * values * (1.0 + jnp.tanh(GELU_SCALE * (values + 0.044715 * values * values * values)))

def matmul(left, right):
    return jnp.dot(left, right, precision=HIGH, preferred_element_type=jnp.float32)

def segments_of(seq_lengths):
    ends = jnp.cumsum(seq_lengths, axis=1)
    position = jnp.arange(TOK_DEV, dtype=jnp.int32)
    return lax.optimization_barrier(jnp.sum((position[None, :, None] >= ends[:, None, :]).astype(jnp.int32), axis=2))

def attend_buffer(items):
    queries, keys, values, segment = items
    scores = low_back(SCORE_SCALE * jnp.einsum('qhe,khe->hqk', queries, keys, precision=HIGH))
    position = jnp.arange(TOK_DEV, dtype=jnp.int32)
    allowed = (segment[:, None] == segment[None, :]) & (position[None, :] <= position[:, None])
    scores = jnp.where(allowed[None], scores, jnp.float32(-1e+30))
    row_max = lax.optimization_barrier(jnp.max(scores, axis=-1, keepdims=True))
    expd = jnp.exp(scores - row_max)
    probs = expd / lax.optimization_barrier(jnp.sum(expd, axis=-1, keepdims=True))
    return jnp.einsum('hqk,khe->qhe', low(probs), values, precision=HIGH)

def forward(segment, inputs, ln1_gain, ln1_bias, w_qkv, qv_bias, w_out, out_bias, ln2_gain, ln2_bias, w_fc, fc_bias, w_proj, proj_bias):
    normed_one = low(layer_norm(inputs, ln1_gain, ln1_bias))
    queries = low_back(low(matmul(normed_one, w_qkv[0]) + qv_bias[0]))
    keys = low_back(low(matmul(normed_one, w_qkv[1])))
    values = low_back(low(matmul(normed_one, w_qkv[2]) + qv_bias[1]))
    shape = (N_DP, TOK_DEV, HEADS, HEAD_DIM)
    attended = lax.map(jax.checkpoint(attend_buffer), (queries.reshape(shape), keys.reshape(shape), values.reshape(shape), segment))
    attended = low_back(low(attended.reshape(TOKENS, D)))
    branch = low_back(matmul(attended, w_out) + out_bias)
    residual = inputs + branch
    normed_two = low(layer_norm(residual, ln2_gain, ln2_bias))
    hidden_pre = low_back(matmul(normed_two, w_fc) + fc_bias)
    hidden = low(gelu(hidden_pre))
    mlp_out = low_back(matmul(hidden, w_proj) + proj_bias)
    return residual + mlp_out

def reference(block_input, cotangent, seq_lengths, ln1_gain, ln1_bias, w_qkv, qv_bias, w_out, out_bias, ln2_gain, ln2_bias, w_fc, fc_bias, w_proj, proj_bias):
    segment = segments_of(seq_lengths)
    valid = (segment < SEQ_DEV).astype(jnp.float32).reshape(TOKENS, 1)
    primals = (block_input.astype(jnp.float32), ln1_gain, ln1_bias, w_qkv.astype(jnp.float32), qv_bias, w_out.astype(jnp.float32), out_bias, ln2_gain, ln2_bias, w_fc.astype(jnp.float32), fc_bias, w_proj.astype(jnp.float32), proj_bias)
    output, pullback = jax.vjp(partial(forward, segment), *primals)
    grads = pullback(cotangent.astype(jnp.float32) * valid)
    return (output.astype(jnp.bfloat16), grads[0].astype(jnp.bfloat16), grads[1], grads[2], grads[3], grads[4], grads[5], grads[6], grads[7], grads[8], grads[9], grads[10], grads[11], grads[12])
```

```python
import functools

import jax
import jax.numpy as jnp
from jax import lax
from jax.experimental import pallas as pl
from jax.experimental.pallas import tpu as pltpu
from jax.sharding import PartitionSpec as P

HEAD_DIM = 64


EPS = 1e-05
GELU_SCALE = 0.7978845608028654
SCORE_SCALE = 0.125


def layer_norm(values, gain, shift):
    centre = jnp.mean(values, axis=-1, keepdims=True)
    centred = values - centre
    spread = jnp.mean(centred * centred, axis=-1, keepdims=True)
    return centred * lax.rsqrt(spread + EPS) * gain + shift


def gelu(values):
    return (
        0.5 * values * (1.0 + jnp.tanh(GELU_SCALE * (values + 0.044715 * values * values * values)))
    )


MESH = pl.DeviceIdType.MESH
CUTS = 4
ORDERS = ("xyz", "yzx", "zxy", "zxy", "xyz")
PIECES = (CUTS, CUTS, CUTS, CUTS, 1)


class Stream:
    def __init__(self, shape, order, pieces):
        self.order, self.pieces = order, pieces
        self.cell_rows = shape[0] // 8
        self.rows = self.cell_rows // pieces
        self.columns = shape[1]
        self.slots = [
            (2 if axis == "z" else 1) * 2 ** (2 - step) for step, axis in enumerate(order)
        ]
        self.held = 8 if order[0] == "z" else 4
        self.offsets = []
        total = 0
        for _ in range(2):
            for count in self.slots:
                self.offsets.append(total)
                total += count * pieces
        self.semaphores = total

    def scratch(self):
        shape = (self.cell_rows, self.columns)
        return (
            [pltpu.VMEM((self.held,) + shape, jnp.float32)]
            + [pltpu.VMEM((count,) + shape, jnp.float32) for count in self.slots]
            + [
                pltpu.SemaphoreType.DMA((self.semaphores,)),
                pltpu.SemaphoreType.DMA((self.semaphores,)),
                pltpu.SemaphoreType.DMA((self.held,)),
                pltpu.SemaphoreType.DMA((self.pieces,)),
            ]
        )

    def bind(self, source, result, held, one, two, three, send, recv, load, store):
        self.source, self.result, self.acc = source, result, held
        self.landing = (one, two, three)
        self.send, self.recv, self.load, self.store = send, recv, load, store


def reduce_kernel(streams, *refs):
    count = len(streams)
    for number, stream in enumerate(streams):
        first = 2 * count + 8 * number
        stream.bind(refs[number], refs[count + number], *refs[first : first + 8])
    me = lax.axis_index("dp")
    other_axis = lax.axis_index("tensor")
    x, y, z = lax.rem(me, 2), lax.rem(me // 2, 2), me // 4
    mine = {"x": x, "y": y, "z": z // 2}
    other = {"x": 1 - x, "y": 1 - y}
    below, above = me - 4, me + 4
    partner = {"x": me + 1 - 2 * x, "y": me + 2 - 4 * y}
    at_end = (z == 0) | (z == 3)
    inside = (z == 1) | (z == 2)
    at = {0: z == 0, 1: z == 3}
    away = {0: z != 0, 1: z != 3}
    drains = []

    def device(index):
        return (index, other_axis)

    def span(stream, k):
        start = k * stream.rows
        return pl.ds(pl.multiple_of(start, 8), stream.rows)

    def in_hbm(stream, ref, bits, k):
        cell = 4 * bits["x"] + 2 * bits["y"] + bits["z"]
        start = cell * stream.cell_rows + k * stream.rows
        return ref.at[pl.ds(pl.multiple_of(start, 8), stream.rows)]

    def held_slot(stream, bits):
        a, b, c = stream.order
        low = 2 * bits[b] + bits[c]
        return 4 * bits[a] + low if stream.held == 8 else low

    def in_acc(stream, bits, k):
        return stream.acc.at[held_slot(stream, bits), span(stream, k)]

    def step_slot(stream, step, bits):
        slot = 0
        for axis in stream.order[step + 1 :]:
            slot = 2 * slot + bits[axis]
        if stream.order[step] == "z":
            slot = slot + bits["z"] * 2 ** (2 - step)
        return slot

    def landing(stream, step, bits, k):
        return stream.landing[step].at[step_slot(stream, step, bits), span(stream, k)]

    def remote(stream, phase, step, bits, k, src, dst, to):
        index = stream.offsets[3 * phase + step] + step_slot(stream, step, bits) * stream.pieces + k
        return pltpu.make_async_remote_copy(
            src_ref=src,
            dst_ref=dst,
            send_sem=stream.send.at[index],
            recv_sem=stream.recv.at[index],
            device_id=device(to),
            device_id_type=MESH,
        )

    def guarded(condition, work):
        if condition is None:
            work()
        else:
            pl.when(condition)(work)

    def scatter_copy(stream, step, bits, from_input):
        axis = stream.order[step]
        to = partner[axis] if axis != "z" else (below if bits["z"] == 0 else above)

        def make(k):
            src = in_hbm(stream, stream.source, bits, k) if from_input else in_acc(stream, bits, k)
            return remote(stream, 0, step, bits, k, src, landing(stream, step, bits, k), to)

        return make

    def gather_copy(stream, step, bits, from_acc):
        axis = stream.order[step]
        to = partner[axis] if axis != "z" else (above if bits["z"] == 0 else below)

        def make(k):
            dst = in_hbm(stream, stream.result, bits, k)
            src = in_acc(stream, bits, k) if from_acc else in_hbm(stream, stream.result, bits, k)
            return remote(stream, 1, step, bits, k, src, dst, to)

        return make

    def later_bits(stream, step):
        settings = [({}, {})]
        for axis in stream.order[step + 1 :]:
            grown = []
            for bits, tags in settings:
                for tag in (1, 0):
                    if axis == "z":
                        value = 1 - tag
                    else:
                        value = other[axis] if tag else mine[axis]
                    grown.append(({**bits, axis: value}, {**tags, axis: tag}))
            settings = grown
        return settings

    def full(stream, step, later):
        bits = {axis: mine[axis] for axis in stream.order[:step]}
        return {**bits, **later}

    def only_ends(stream, step):
        return at_end if "z" in stream.order[:step] else None

    def send(stream, k, make, condition):
        guarded(condition, lambda: make(k).start())
        drains.append((stream.pieces, make, condition))

    def ready(stream, step, bits, tags, k, condition):
        if step == 3:
            own = pltpu.make_async_copy(
                in_acc(stream, bits, k),
                in_hbm(stream, stream.result, bits, k),
                stream.store.at[k],
            )
            guarded(condition, own.start)
            for ahead in (2, 1, 0):
                if stream.order[ahead] != "z":
                    send(stream, k, gather_copy(stream, ahead, bits, True), condition)
                else:
                    for end in (0, 1):
                        cell = {**bits, "z": end}
                        send(stream, k, gather_copy(stream, ahead, cell, True), at[end])
            return
        axis = stream.order[step]
        if axis == "z":
            end = bits["z"]
            send(stream, k, scatter_copy(stream, step, bits, False), at[1 - end])
        elif tags[axis]:
            send(stream, k, scatter_copy(stream, step, bits, False), condition)

    def add_landed(stream, step, bits, k):
        remote(
            stream, 0, step, bits, k, in_acc(stream, bits, k), landing(stream, step, bits, k), me
        ).wait_recv()
        slot, place = held_slot(stream, bits), step_slot(stream, step, bits)

        @pl.loop(0, stream.rows // 8)
        def _(row):
            rows = pl.ds(pl.multiple_of(k * stream.rows + row * 8, 8), 8)
            stream.acc[slot, rows] = stream.acc[slot, rows] + stream.landing[step][place, rows]

    def scatter(stream, step, later, tags, k):
        axis = stream.order[step]
        ends = only_ends(stream, step)
        if axis != "z":
            bits = full(stream, step, {**later, axis: mine[axis]})
            guarded(ends, lambda: add_landed(stream, step, bits, k))
            ready(stream, step + 1, bits, tags, k, ends)
            return
        for end in (0, 1):
            bits = full(stream, step, {**later, "z": end})
            guarded(away[1 - end], lambda bits=bits: add_landed(stream, step, bits, k))
            send(stream, k, scatter_copy(stream, step, bits, False), inside)
        if step == 2:
            bits = full(stream, step, {**later, "z": mine["z"]})
            ready(stream, 3, bits, tags, k, at_end)
        else:
            for end in (0, 1):
                axis = stream.order[step + 1]
                if tags[axis]:
                    bits = full(stream, step, {**later, "z": end})
                    send(stream, k, scatter_copy(stream, step + 1, bits, False), at[end])

    def gather(stream, step, later, k):
        axis = stream.order[step]
        ends = only_ends(stream, step)

        def landed(bits):
            here = in_hbm(stream, stream.result, bits, k)
            remote(stream, 1, step, bits, k, here, here, me).wait_recv()

        def onward(bits, condition):
            for ahead in range(step - 1, -1, -1):
                if stream.order[ahead] != "z":
                    send(stream, k, gather_copy(stream, ahead, bits, False), condition)
                else:
                    for end in (0, 1):
                        cell = {**bits, "z": end}
                        send(stream, k, gather_copy(stream, ahead, cell, False), at[end])

        if axis != "z":
            bits = full(stream, step, {**later, axis: other[axis]})
            guarded(ends, lambda: landed(bits))
            onward(bits, ends)
            return
        for end in (0, 1):
            bits = full(stream, step, {**later, "z": end})
            guarded(away[end], lambda bits=bits: landed(bits))
            send(stream, k, gather_copy(stream, step, bits, False), inside)
            onward(bits, away[end])

    def loads(stream):
        a, b, c = stream.order
        for slot in range(stream.held):
            bits = {b: (slot // 2) % 2, c: slot % 2, a: slot // 4 if stream.held == 8 else mine[a]}
            cell = 4 * bits["x"] + 2 * bits["y"] + bits["z"]
            start = pl.multiple_of(cell * stream.cell_rows, 8)
            yield pltpu.make_async_copy(
                stream.source.at[pl.ds(start, stream.cell_rows)],
                stream.acc.at[slot],
                stream.load.at[slot],
            )

    barrier = pltpu.get_barrier_semaphore()

    def greet(index):
        pl.semaphore_signal(barrier, inc=1, device_id=device(index), device_id_type=MESH)

    for stream in streams:
        for copy in loads(stream):
            copy.start()
    greet(partner["x"])
    greet(partner["y"])
    pl.when(z > 0)(lambda: greet(below))
    pl.when(z < 3)(lambda: greet(above))
    pl.semaphore_wait(barrier, 3 + inside.astype(jnp.int32))

    big = [stream for stream in streams if stream.pieces > 1]
    little = [stream for stream in streams if stream.pieces == 1]

    def each(step, work):
        settings = {id(stream): later_bits(stream, step) for stream in streams}
        for turn in range(2 ** (2 - step)):
            for stream in little:
                work(stream, step, *settings[id(stream)][turn], 0)

            @pl.loop(0, CUTS)
            def _(k):
                for stream in big:
                    work(stream, step, *settings[id(stream)][turn], k)

    def first(stream, step, later, tags, k):
        axis = stream.order[0]
        if axis == "z":
            for end in (0, 1):
                bits = {**later, "z": end}
                send(stream, k, scatter_copy(stream, 0, bits, True), at[1 - end])
        else:
            bits = {**later, axis: other[axis]}
            send(stream, k, scatter_copy(stream, 0, bits, True), None)

    each(0, first)
    for stream in streams:
        for copy in loads(stream):
            copy.wait()
    for step in (0, 1, 2):
        each(step, scatter)
    for step in (2, 1, 0):
        each(step, lambda stream, step, later, tags, k: gather(stream, step, later, k))

    for pieces, make, condition in drains:

        def drain(pieces=pieces, make=make):
            @pl.loop(0, pieces)
            def _(k):
                make(k).wait_send()

        guarded(condition, drain)
    for stream in streams:
        bits = dict(mine)

        def stored(stream=stream, bits=bits):
            @pl.loop(0, stream.pieces)
            def _(k):
                pltpu.make_async_copy(
                    in_acc(stream, bits, k),
                    in_hbm(stream, stream.result, bits, k),
                    stream.store.at[k],
                ).wait()

        pl.when(at_end)(stored)


def sum_over_data(arrays):
    streams = [
        Stream(item.shape, order, pieces)
        for item, order, pieces in zip(arrays, ORDERS, PIECES, strict=True)
    ]
    size = sum(item.size for item in arrays)
    return pl.pallas_call(
        functools.partial(reduce_kernel, streams),
        out_shape=[jax.ShapeDtypeStruct(item.shape, item.dtype) for item in arrays],
        in_specs=[pl.BlockSpec(memory_space=pl.ANY)] * len(arrays),
        out_specs=[pl.BlockSpec(memory_space=pl.ANY)] * len(arrays),
        scratch_shapes=[piece for stream in streams for piece in stream.scratch()],
        compiler_params=pltpu.CompilerParams(
            collective_id=0, has_side_effects=True, vmem_limit_bytes=52 * 2**20
        ),
        cost_estimate=pl.CostEstimate(
            flops=2 * size, bytes_accessed=8 * size, transcendentals=0
        ),
    )(*arrays)


def sum_gradients(w_qkv_grad, w_out_grad, w_fc_grad, w_proj_grad, vectors):
    if lax.axis_size("dp") != 16:
        return lax.psum((w_qkv_grad, w_out_grad, w_fc_grad, w_proj_grad, vectors), "dp")
    flat = jnp.concatenate([item.reshape(-1, 128) for item in vectors])
    rows = flat.shape[0]
    flat = jnp.pad(flat, ((0, -rows % 64), (0, 0)))
    stacked = w_qkv_grad.reshape(-1, w_qkv_grad.shape[2])
    proj, fc, qkv, out, flat = sum_over_data([w_proj_grad, w_fc_grad, stacked, w_out_grad, flat])
    summed, start = [], 0
    for item in vectors:
        height = item.size // 128
        summed.append(flat[start : start + height].reshape(item.shape))
        start += height
    return qkv.reshape(w_qkv_grad.shape), out, fc, proj, summed


def per_device(
    block_input,
    cotangent,
    seq_lengths,
    ln1_gain,
    ln1_bias,
    w_qkv,
    qv_bias,
    w_out,
    out_bias,
    ln2_gain,
    ln2_bias,
    w_fc,
    fc_bias,
    w_proj,
    proj_bias,
):
    rows = block_input.shape[0]
    local_width = w_qkv.shape[2]
    heads = local_width // HEAD_DIM
    ends = jnp.cumsum(seq_lengths[0])
    position = jnp.arange(rows, dtype=jnp.int32)
    segment = jnp.sum((position[:, None] >= ends[None, :]).astype(jnp.int32), axis=1)
    valid = (segment < seq_lengths.shape[1]).astype(jnp.float32)
    inputs = block_input.astype(jnp.float32)
    normed_one = layer_norm(inputs, ln1_gain, ln1_bias).astype(jnp.bfloat16)
    projected = jnp.einsum("td,cdh->cth", normed_one, w_qkv, preferred_element_type=jnp.float32)
    queries = (projected[0] + qv_bias[0]).astype(jnp.bfloat16)
    keys = projected[1].astype(jnp.bfloat16)
    values = (projected[2] + qv_bias[1]).astype(jnp.bfloat16)
    query_heads = queries.reshape(rows, heads, HEAD_DIM)
    key_heads = keys.reshape(rows, heads, HEAD_DIM)
    value_heads = values.reshape(rows, heads, HEAD_DIM)

    def scores_of():
        scores = (
            jnp.einsum("qhe,khe->hqk", query_heads, key_heads, preferred_element_type=jnp.float32)
            * SCORE_SCALE
        )
        allowed = (segment[:, None] == segment[None, :]) & (position[None, :] <= position[:, None])
        return jnp.where(allowed[None], scores, jnp.float32(-1e30))

    scores = scores_of()
    row_max = jnp.max(scores, axis=-1, keepdims=True)
    expd = jnp.exp(scores - row_max)
    total = jnp.sum(expd, axis=-1, keepdims=True)
    probs = expd / total
    log_totals = row_max + jnp.log(total)
    pieces = jnp.einsum(
        "hqk,khe->qhe", probs.astype(jnp.bfloat16), value_heads, preferred_element_type=jnp.float32
    )
    attended = pieces.reshape(rows, local_width).astype(jnp.bfloat16)
    branch = (
        lax.psum(jnp.dot(attended, w_out, preferred_element_type=jnp.float32), "tensor") + out_bias
    )
    residual = inputs + branch
    normed_two = layer_norm(residual, ln2_gain, ln2_bias).astype(jnp.bfloat16)
    hidden_pre = jnp.dot(normed_two, w_fc, preferred_element_type=jnp.float32) + fc_bias
    hidden = gelu(hidden_pre).astype(jnp.bfloat16)
    mlp_out = (
        lax.psum(jnp.dot(hidden, w_proj, preferred_element_type=jnp.float32), "tensor") + proj_bias
    )
    block_output = (residual + mlp_out).astype(jnp.bfloat16)
    grad_out = cotangent.astype(jnp.float32) * valid[:, None]
    grad_mlp = grad_out.astype(jnp.bfloat16)
    proj_bias_grad = jnp.sum(grad_mlp.astype(jnp.float32), axis=0)
    w_proj_grad = jnp.einsum("tf,td->fd", hidden, grad_mlp, preferred_element_type=jnp.float32)
    grad_act = jnp.einsum("td,fd->tf", grad_mlp, w_proj, preferred_element_type=jnp.float32)
    grad_hidden = jax.vjp(gelu, hidden_pre)[1](grad_act)[0].astype(jnp.bfloat16)
    fc_bias_grad = jnp.sum(grad_hidden.astype(jnp.float32), axis=0)
    w_fc_grad = jnp.einsum("td,tf->df", normed_two, grad_hidden, preferred_element_type=jnp.float32)
    grad_normed_two = lax.psum(
        jnp.einsum("tf,df->td", grad_hidden, w_fc, preferred_element_type=jnp.float32), "tensor"
    )
    grad_res_ln, ln2_gain_grad, ln2_bias_grad = jax.vjp(layer_norm, residual, ln2_gain, ln2_bias)[
        1
    ](grad_normed_two)
    grad_residual = grad_out + grad_res_ln
    grad_branch = grad_residual.astype(jnp.bfloat16)
    out_bias_grad = jnp.sum(grad_branch.astype(jnp.float32), axis=0)
    w_out_grad = jnp.einsum("th,td->hd", attended, grad_branch, preferred_element_type=jnp.float32)
    grad_attended = jnp.einsum("td,hd->th", grad_branch, w_out, preferred_element_type=jnp.float32)
    grad_attended = grad_attended.astype(jnp.bfloat16).reshape(rows, heads, HEAD_DIM)
    probs = jnp.exp(scores_of() - log_totals)
    grad_probs = jnp.einsum(
        "qhe,khe->hqk", grad_attended, value_heads, preferred_element_type=jnp.float32
    )
    inner = jnp.sum(probs * grad_probs, axis=-1, keepdims=True)
    grad_scores = (probs * (grad_probs - inner)).astype(jnp.bfloat16)
    query_pieces = (
        jnp.einsum("hqk,khe->qhe", grad_scores, key_heads, preferred_element_type=jnp.float32)
        * SCORE_SCALE
    )
    grad_keys = (
        jnp.einsum("hqk,qhe->khe", grad_scores, query_heads, preferred_element_type=jnp.float32)
        * SCORE_SCALE
    )
    grad_values = jnp.einsum(
        "hqk,qhe->khe",
        probs.astype(jnp.bfloat16),
        grad_attended,
        preferred_element_type=jnp.float32,
    )
    grad_queries = query_pieces.reshape(rows, local_width).astype(jnp.bfloat16)
    grad_keys = grad_keys.reshape(rows, local_width).astype(jnp.bfloat16)
    grad_values = grad_values.reshape(rows, local_width).astype(jnp.bfloat16)
    grad_stack = jnp.stack([grad_queries, grad_keys, grad_values], axis=0)
    qv_bias_grad = jnp.stack(
        [
            jnp.sum(grad_queries.astype(jnp.float32), axis=0),
            jnp.sum(grad_values.astype(jnp.float32), axis=0),
        ],
        axis=0,
    )
    w_qkv_grad = jnp.einsum(
        "td,cth->cdh", normed_one, grad_stack, preferred_element_type=jnp.float32
    )
    grad_normed_one = lax.psum(
        jnp.einsum("cth,cdh->td", grad_stack, w_qkv, preferred_element_type=jnp.float32), "tensor"
    )
    grad_in_ln, ln1_gain_grad, ln1_bias_grad = jax.vjp(layer_norm, inputs, ln1_gain, ln1_bias)[1](
        grad_normed_one
    )
    input_grad = (grad_residual + grad_in_ln).astype(jnp.bfloat16)
    vectors = [
        ln1_gain_grad,
        ln1_bias_grad,
        qv_bias_grad,
        out_bias_grad,
        ln2_gain_grad,
        ln2_bias_grad,
        fc_bias_grad,
        proj_bias_grad,
    ]
    w_qkv_grad, w_out_grad, w_fc_grad, w_proj_grad, vectors = sum_gradients(
        w_qkv_grad, w_out_grad, w_fc_grad, w_proj_grad, vectors
    )
    return (
        block_output,
        input_grad,
        vectors[0],
        vectors[1],
        w_qkv_grad,
        vectors[2],
        w_out_grad,
        vectors[3],
        vectors[4],
        vectors[5],
        w_fc_grad,
        vectors[6],
        w_proj_grad,
        vectors[7],
    )


def solution(mesh):
    return jax.shard_map(
        per_device,
        mesh=mesh,
        in_specs=(
            P("dp", None),
            P("dp", None),
            P("dp", None),
            P(),
            P(),
            P(None, None, "tensor"),
            P(None, "tensor"),
            P("tensor", None),
            P(),
            P(),
            P(),
            P(None, "tensor"),
            P("tensor"),
            P("tensor", None),
            P(),
        ),
        out_specs=(
            P("dp", None),
            P("dp", None),
            P(),
            P(),
            P(None, None, "tensor"),
            P(None, "tensor"),
            P("tensor", None),
            P(),
            P(),
            P(),
            P(None, "tensor"),
            P("tensor"),
            P("tensor", None),
            P(),
        ),
        check_vma=False,
    )
```
